32 devices in a mesh: space: 8 (over z, x), vel: 4 (over y, core).
Axes of the slice: x: 2, y: 2, z: 4, core: 2. Of those that a mesh axis runs over, the one named last changes fastest.
Arguments:
- velocity_dist: bfloat16 [32768, 2048], P('vel', 'space'), may hold values from -6 to 6
- macro_state: float32 [13, 2048], P(None, ('space', 'vel')), may hold values from -2 to 2
- collision_rate: float32 [2048], P('space'), may hold values from 0.25 to 2
- wall_flags: int32 [2048], P('space'), may hold values 0 or 1
- diffusivity: float32 [13], replicated, may hold values from 0.5 to 8
- coupling: float32 [13, 13], replicated, may hold values from -0.25 to 4.5, as said below
Outputs:
- dist_out: bfloat16 [32768, 2048], P('vel', 'space')
- macro_out: float32 [13, 2048], P(None, ('space', 'vel'))
The draws below stay inside these ranges and needn't reach their ends.
Inputs may be any that keep to these rules, and one draw needn't show every extreme that they name: `coupling`: symmetric, with each diagonal entry larger than the sum of magnitudes of the other entries of its row.
All inputs are finite; a program needn't handle non-finite values. No bound on the sum of `wall_flags` on one device may be relied on, other than what follows from the above.
Results may differ from the reference program's by a relative error of at most 0.001.
Values sent between devices are 32-bit elements; how exact they have to be, the bound alone decides.
A program may use at most 64 MiB of HBM per device.

```python
import math
import jax
import jax.numpy as jnp
from jax import lax

NV1 = 32
VEL = 32768
K = 13
ITERS = 3
SWEEPS = 2
NX = 2048
N_VEL = 4


def draw_coupling(key, part):
    spread = 0.15
    perturb = jax.random.uniform(jax.random.fold_in(key, 11), (K, K), jnp.float32, -spread, spread)
    symmetric = 0.5 * (perturb + perturb.T)
    offdiag = symmetric * (1.0 - jnp.eye(K, dtype=jnp.float32))
    margin = jax.random.uniform(jax.random.fold_in(key, 12), (K,), jnp.float32, 0.5, 1.5)
    diagonal = jnp.sum(jnp.abs(offdiag), axis=1) + margin
    return offdiag + jnp.diag(diagonal)


def touch_ends(drawn, own_key, least, high):
    longest = drawn.shape.index(max(drawn.shape))
    spots = []
    for shift in (0, 1):
        where = [jax.random.randint(jax.random.fold_in(own_key, axis), (), 0, length) for axis, length in enumerate(drawn.shape)]
        where[longest] = (where[longest] + shift) % drawn.shape[longest]
        spots.append(tuple(where))
    return drawn.at[spots[0]].set(least).at[spots[1]].set(high)


def steps_of(rng, shape, cuts, smallest, top_value):
    loudness, own = 1.0, jax.random.fold_in(rng, 6)
    for position, shards_of in cuts:
        draws = jnp.exp(jax.random.uniform(jax.random.fold_in(own, position), (shards_of,), jnp.float32, smallest / len(cuts), top_value / len(cuts)))
        loudness = loudness * jnp.repeat(draws, shape[position] // shards_of).reshape([-1 if axis == position else 1 for axis in range(len(shape))])
    return loudness


def scatter_about(key, extent, scale, bound, cuts=(), kind=jnp.bfloat16):
    values = scale * jax.random.normal(key, extent, jnp.float32)
    if cuts:
        values = values * steps_of(key, extent, cuts, -0.22, 0.18)
    return jnp.clip(values, -bound, bound).astype(kind)


def setup_inputs(seed: int = 0) -> dict:
    keys = jax.random.split(jax.random.key(seed), 7)
    return {
        "velocity_dist": scatter_about(keys[0], (VEL, NX), 1.0, 6.0, ((0, 4), (1, 8))),
        "macro_state": scatter_about(keys[1], (K, NX), 0.3, 2.0, ((1, 32),), jnp.float32),
        "collision_rate": jnp.clip(jnp.exp(math.log(2.0) - 2.0794415 * jax.random.uniform(keys[2], (NX,), jnp.float32) ** steps_of(keys[2], (NX,), ((0, 8),), -0.2, 0.2)), 0.25, 2.0),
        "wall_flags": touch_ends((jax.random.randint(keys[3], (NX,), 0, 8) < 1).astype(jnp.int32), jax.random.fold_in(keys[3], 1), 0, 1),
        "diffusivity": jnp.clip(jnp.exp(jax.random.uniform(keys[4], (K,), jnp.float32, math.log(0.5), math.log(8.0))), 0.5, 8.0),
        "coupling": draw_coupling(jax.random.fold_in(keys[6], 71), 0),
    }


highest = lax.Precision.HIGHEST
speed_limit = 4.0
time_step = 0.125
shakhov_weights = (1.0, 1.0, 1.0, 1.0, 1.0, 0.0, 0.0, 0.0, 0.0, 0.0, 1.0 / 3.0, 1.0 / 3.0, 1.0 / 3.0)

def velocity_table(first_row, number):
    indices = first_row + jnp.arange(number, dtype=jnp.int32)
    first_index = indices // (NV1 * NV1)
    second_index = indices // NV1 % NV1
    third_index = indices % NV1
    spacing = 2.0 * speed_limit / NV1
    speed_x = (first_index.astype(jnp.float32) + 0.5) * spacing - speed_limit
    speed_y = (second_index.astype(jnp.float32) + 0.5) * spacing - speed_limit
    speed_z = (third_index.astype(jnp.float32) + 0.5) * spacing - speed_limit
    speed_square = speed_x * speed_x + speed_y * speed_y + speed_z * speed_z
    weight = jnp.exp(-0.5 * speed_square) * (spacing ** 3 / (2.0 * math.pi) ** 1.5)
    return (speed_x, speed_y, speed_z, weight)

def moment_basis(speed_x, speed_y, speed_z):
    speed_square = speed_x * speed_x + speed_y * speed_y + speed_z * speed_z
    entries = [jnp.ones_like(speed_x), speed_x, speed_y, speed_z, (speed_square - 3.0) / math.sqrt(6.0), speed_x * speed_y, speed_x * speed_z, speed_y * speed_z, 0.5 * (speed_x * speed_x - speed_y * speed_y), (speed_x * speed_x + speed_y * speed_y - 2.0 * speed_z * speed_z) / math.sqrt(12.0), speed_x * (speed_square - 5.0) / math.sqrt(10.0), speed_y * (speed_square - 5.0) / math.sqrt(10.0), speed_z * (speed_square - 5.0) / math.sqrt(10.0)]
    return jnp.stack(entries)

def apply_operator(moments, diffusivity, coupling):
    padded = jnp.pad(moments, ((0, 0), (1, 1)))
    second_diff = 2.0 * moments - padded[:, :-2] - padded[:, 2:]
    return jnp.dot(coupling, moments, precision=highest) + diffusivity[:, None] * second_diff

def synthetic(residual, diffusivity, coupling):
    result = jnp.zeros_like(residual)
    for repeat in range(SWEEPS):
        applied = apply_operator(residual, diffusivity, coupling)
        step_size = jnp.sum(residual * residual) / jnp.sum(residual * applied)
        result = result + step_size * residual
        residual = residual - step_size * applied
    return result

def reference(velocity_dist, macro_state, collision_rate, wall_flags, diffusivity, coupling):
    total_rows = velocity_dist.shape[0]
    cell_count = velocity_dist.shape[1]
    blocks = N_VEL
    block_rows = total_rows // blocks
    relax_rate = time_step * collision_rate * (1.0 + wall_flags.astype(jnp.float32))
    shakhov = jnp.array(shakhov_weights, dtype=jnp.float32)
    distribution = velocity_dist.astype(jnp.float32).reshape(blocks, block_rows, cell_count)
    starts = jnp.arange(blocks, dtype=jnp.int32) * block_rows
    current = macro_state
    for iteration in range(ITERS):

        def kinetic(pieces):
            velocity_block, first_row = pieces
            speed_x, speed_y, speed_z, weight = velocity_table(first_row, block_rows)
            basis_rows = moment_basis(speed_x, speed_y, speed_z)
            equilibrium = jnp.dot((basis_rows * shakhov[:, None]).T, current, precision=highest)
            padded = jnp.pad(velocity_block, ((0, 0), (1, 1)))
            gradient = jnp.where((speed_x > 0.0)[:, None], velocity_block - padded[:, :-2], padded[:, 2:] - velocity_block)
            advanced = velocity_block - (time_step * speed_x)[:, None] * gradient + relax_rate[None, :] * (equilibrium - velocity_block)
            partial_value = jnp.dot(basis_rows * weight[None, :], advanced, precision=highest)
            return (advanced, partial_value)
        halves, partials = lax.map(kinetic, (distribution, starts))
        shares = lax.optimization_barrier(jnp.sum(partials, axis=0))
        correction = synthetic(shares - current, diffusivity, coupling)
        current = shares + correction

        def correct(pieces):
            velocity_block, first_row = pieces
            speed_x, speed_y, speed_z, weight = velocity_table(first_row, block_rows)
            basis_rows = moment_basis(speed_x, speed_y, speed_z)
            return velocity_block + jnp.dot(basis_rows.T, correction, precision=highest)
        distribution = lax.map(correct, (halves, starts))
    return (distribution.reshape(total_rows, cell_count).astype(jnp.bfloat16), current)
```

```python
import math

import jax
import jax.numpy as jnp
import numpy as np
from jax import lax
from jax.experimental import pallas as pl
from jax.experimental.pallas import tpu as pltpu
from jax.sharding import PartitionSpec as P

NV1 = 32
ITERS = 3
SWEEPS = 2
K = 13
Q = 8
HALO = 8
TILE = 128
MESH = pl.DeviceIdType.MESH

speed_limit = 4.0
time_step = 0.125
shakhov_weights = (1.0,) * 5 + (0.0,) * 5 + (1.0 / 3.0,) * 3


def two_parts(x):
    high = np.asarray(x, np.float32).astype(jnp.bfloat16)
    low = (np.asarray(x, np.float32) - high.astype(np.float32)).astype(jnp.bfloat16)
    return high, low


def tables():
    spacing = 2.0 * speed_limit / NV1
    v = (np.arange(NV1) + 0.5) * spacing - speed_limit
    w1 = np.exp(-0.5 * v * v) * spacing / math.sqrt(2.0 * math.pi)
    y = np.repeat(v, NV1)
    z = np.tile(v, NV1)
    w_yz = np.repeat(w1, NV1) * np.tile(w1, NV1)
    phi = np.stack([np.ones_like(y), y, z, y * y, z * z, y * z, y * (y * y + z * z), z * (y * y + z * z)])
    beta = np.zeros((NV1, Q, 16))
    r6, r12, r10 = math.sqrt(6.0), math.sqrt(12.0), math.sqrt(10.0)
    beta[:, 0, 0] = 1.0
    beta[:, 0, 1] = v
    beta[:, 1, 2] = 1.0
    beta[:, 2, 3] = 1.0
    beta[:, 0, 4], beta[:, 3, 4], beta[:, 4, 4] = (v * v - 3.0) / r6, 1.0 / r6, 1.0 / r6
    beta[:, 1, 5] = v
    beta[:, 2, 6] = v
    beta[:, 5, 7] = 1.0
    beta[:, 0, 8], beta[:, 3, 8] = 0.5 * v * v, -0.5
    beta[:, 0, 9], beta[:, 3, 9], beta[:, 4, 9] = v * v / r12, 1.0 / r12, -2.0 / r12
    beta[:, 0, 10], beta[:, 3, 10], beta[:, 4, 10] = v * (v * v - 5.0) / r10, v / r10, v / r10
    beta[:, 1, 11], beta[:, 6, 11] = (v * v - 5.0) / r10, 1.0 / r10
    beta[:, 2, 12], beta[:, 7, 12] = (v * v - 5.0) / r10, 1.0 / r10
    gram = (phi * w_yz) @ phi.T
    rows = NV1 * Q
    project = np.einsum("qr,vrk->vqk", gram, beta).reshape(rows, 16)
    moments = (w1[:, None, None] * beta).reshape(rows, 16).T
    inner = moments @ project

    def left(a):
        high, low = two_parts(a)
        return np.concatenate([high, high, low], axis=1)

    reduce_h, reduce_l = two_parts(phi * w_yz)
    phi_h, phi_l = two_parts(phi)
    m_h, m_l = two_parts(moments)
    return dict(
        reduce=np.concatenate([reduce_h, reduce_l]),
        phi=np.concatenate([phi_h, phi_h, phi_l, phi_l]),
        project=left(project),
        beta=left(beta.reshape(rows, 16)),
        moments=np.concatenate([m_h, m_l]),
        inner=left(inner),
    )


def split(x):
    high = x.astype(jnp.bfloat16)
    return high, (x - high.astype(jnp.float32)).astype(jnp.bfloat16)


def dot(a, b):
    return jnp.dot(a, b, preferred_element_type=jnp.float32)


def dot_parts(left, x):
    high, low = split(x)
    return dot(left, jnp.concatenate([high, low, high], axis=0))


def roll(x, shift):
    return pltpu.roll(x, shift % x.shape[1], 1)


def moments_kernel(
    S, N,
    h_ref, macro_ref, rate_ref, wall_ref, diff_ref, coup_ref,
    reduce_ref, project_ref, beta_ref, moments_ref, inner_ref,
    zc_ref, coef_ref, halo_ref, out_ref,
    h_buf, g_all, cur_stage, cur_peers, cur_left, cur_right,
    pack_l, pack_r, from_left, from_right, edge_send, edge_recv, sums, coup_pad,
    h_sem, g_ssem, g_rsem, c_ssem, c_rsem, cl_ssem, cl_rsem, cr_ssem, cr_rsem,
    pl_ssem, pl_rsem, pr_ssem, pr_rsem, e_ssem, e_rsem, s_ssem, s_rsem,
):
    L = h_ref.shape[1]
    W = L + TILE
    width = macro_ref.shape[1]
    per_tile = TILE // width
    plane = NV1 * NV1
    nvx = h_ref.shape[0] // plane
    R = nvx * Q
    group = edge_send.shape[0]
    members = nvx // group
    s = lax.axis_index("space")
    p = lax.axis_index("vel")
    positive = p >= N // 2
    has_left = s > 0
    has_right = s < S - 1
    f32 = jnp.float32

    for j in range(nvx):
        pltpu.make_async_copy(h_ref.at[pl.ds(j * plane, plane)], h_buf.at[pl.ds(j * plane, plane)], h_sem.at[j]).start()

    cur_left[...] = jnp.zeros_like(cur_left)
    cur_right[...] = jnp.zeros_like(cur_right)
    from_left[...] = jnp.zeros_like(from_left)
    from_right[...] = jnp.zeros_like(from_right)
    edge_recv[...] = jnp.zeros_like(edge_recv)

    barrier = pltpu.get_barrier_semaphore()

    def greet(device):
        pl.semaphore_signal(barrier, inc=1, device_id=device, device_id_type=MESH)

    for k in range(1, N):
        greet((s, lax.rem(p + k, N)))

    @pl.when(has_left)
    def _():
        for q in range(N):
            greet((s - 1, q))

    @pl.when(has_right)
    def _():
        for q in range(N):
            greet((s + 1, q))

    for t in range(S):
        @pl.when((t != s) & (t != s - 1) & (t != s + 1))
        def _():
            greet((t, p))

    beside = has_left.astype(jnp.int32) + has_right.astype(jnp.int32)
    greetings = (N - 1) + N * beside + (S - 1 - beside)

    relax = time_step * rate_ref[...] * (1.0 + wall_ref[...].astype(f32))
    edge_relax = jnp.where(p == 0, relax[:, :TILE], relax[:, L - TILE:])
    cur_stage[...] = jnp.zeros_like(cur_stage)
    cur_stage[0:K, :] = jnp.concatenate([macro_ref[...]] * per_tile, axis=1)
    cur_stage[K:K + 1, :] = edge_relax
    cur_peers[p] = cur_stage[...]
    coup_pad[...] = jnp.zeros_like(coup_pad)
    coup_pad[0:K, 0:K] = coup_ref[...]

    row8 = lax.broadcasted_iota(jnp.int32, (8, L), 0)
    col8 = lax.broadcasted_iota(jnp.int32, (8, L), 1)
    upwind_cell = jnp.where(positive, L - 1 - col8, col8)
    pick = []
    for m in range(members):
        t = row8 - 4 * m
        pick.append(((t == upwind_cell) & (t >= 0) & (t < ITERS)).astype(f32).astype(jnp.bfloat16))

    reduce = reduce_ref[...]
    lane8 = lax.broadcasted_iota(jnp.int32, (8, TILE), 1)
    packed_l = jnp.zeros((8, TILE), f32)
    packed_r = jnp.zeros((8, TILE), f32)

    def cur_copy(dst, ssem, rsem, device):
        return pltpu.make_async_remote_copy(
            src_ref=cur_stage, dst_ref=dst, send_sem=ssem, recv_sem=rsem, device_id=device, device_id_type=MESH)

    def g_copy(g, k):
        rows = pl.ds(pl.multiple_of(p * R + g * members * Q, 8), members * Q)
        return pltpu.make_async_remote_copy(
            src_ref=g_all.at[rows, pl.ds(0, L)], dst_ref=g_all.at[rows, pl.ds(0, L)],
            send_sem=g_ssem.at[g, k], recv_sem=g_rsem.at[g, p],
            device_id=(s, lax.rem(p + k, N)), device_id_type=MESH)

    def edge_copy(g, target):
        return pltpu.make_async_remote_copy(
            src_ref=edge_send.at[g], dst_ref=edge_recv.at[g],
            send_sem=e_ssem.at[g], recv_sem=e_rsem.at[g],
            device_id=(target, p), device_id_type=MESH)

    downwind = jnp.where(positive, s + 1, s - 1)
    has_down = (downwind >= 0) & (downwind < S)
    has_up = jnp.where(positive, s - 1, S - 2 - s) >= 0

    for g in range(group):
        edge = jnp.zeros((8, plane), f32)
        for m in range(members):
            j = g * members + m
            pltpu.make_async_copy(
                h_ref.at[pl.ds(j * plane, plane)], h_buf.at[pl.ds(j * plane, plane)], h_sem.at[j]).wait()
            block = h_buf[j * plane:(j + 1) * plane, :]
            both = dot(reduce, block)
            value = both[:Q] + both[Q:]
            g_all[pl.ds(pl.multiple_of(p * R + j * Q, 8), Q), 0:L] = value
            edge = edge + lax.dot_general(pick[m], block, (((1,), (1,)), ((), ())), preferred_element_type=f32)
            here = (lane8 >= HALO * j) & (lane8 < HALO * (j + 1))
            packed_l = jnp.where(here, roll(value[:, :TILE], HALO * j), packed_l)
            packed_r = jnp.where(here, roll(value[:, L - TILE:], HALO * j - (TILE - HALO)), packed_r)
        edge_send[g] = edge
        if g == 0:
            pl.semaphore_wait(barrier, greetings)
            for k in range(1, N):
                cur_copy(cur_peers.at[p], c_ssem.at[k], c_rsem.at[p], (s, lax.rem(p + k, N))).start()

            @pl.when((p == 0) & has_left)
            def _():
                for q in range(N):
                    cur_copy(cur_right, cr_ssem.at[q], cr_rsem, (s - 1, q)).start()

            @pl.when((p == N - 1) & has_right)
            def _():
                for q in range(N):
                    cur_copy(cur_left, cl_ssem.at[q], cl_rsem, (s + 1, q)).start()

        for k in range(1, N):
            g_copy(g, k).start()

        @pl.when(has_down)
        def _():
            edge_copy(g, downwind).start()

    pack_l[...] = packed_l
    pack_r[...] = packed_r

    def pack_copy(src, dst, ssem, rsem, device):
        return pltpu.make_async_remote_copy(
            src_ref=src, dst_ref=dst.at[p], send_sem=ssem, recv_sem=rsem.at[p], device_id=device, device_id_type=MESH)

    @pl.when(has_left)
    def _():
        for q in range(N):
            pack_copy(pack_l, from_right, pl_ssem.at[q], pl_rsem, (s - 1, q)).start()

    @pl.when(has_right)
    def _():
        for q in range(N):
            pack_copy(pack_r, from_left, pr_ssem.at[q], pr_rsem, (s + 1, q)).start()

    vx_row = lax.broadcasted_iota(jnp.int32, (NV1 * Q, 1), 0) // Q
    c_all = time_step * jnp.abs((vx_row.astype(f32) + 0.5) * (2.0 * speed_limit / NV1) - speed_limit)
    own_row = lax.broadcasted_iota(jnp.int32, (R, 1), 0) // Q + p * nvx
    c_own = time_step * jnp.abs((own_row.astype(f32) + 0.5) * (2.0 * speed_limit / NV1) - speed_limit)
    own_vx = lax.broadcasted_iota(jnp.int32, (nvx, 1), 0) + p * nvx
    c_vx = time_step * jnp.abs((own_vx.astype(f32) + 0.5) * (2.0 * speed_limit / NV1) - speed_limit)
    row16 = lax.broadcasted_iota(jnp.int32, (16, 1), 0)
    diffusion = jnp.zeros((16, 1), f32)
    scale = jnp.zeros((16, 1), f32)
    for k in range(K):
        diffusion = jnp.where(row16 == k, diff_ref[k], diffusion)
        scale = jnp.where(row16 == k, shakhov_weights[k], scale)
    lane = lax.broadcasted_iota(jnp.int32, (1, W), 1)
    cell = jnp.where(lane < L + TILE // 2, lane, lane - W) + s * L
    inside = (cell >= 0) & (cell < S * L)
    lane_t = lax.broadcasted_iota(jnp.int32, (1, TILE), 1)
    coupling = coup_pad[...]

    for k in range(1, N):
        q = lax.rem(p + k, N)
        pltpu.make_async_remote_copy(
            src_ref=cur_stage, dst_ref=cur_peers.at[q], send_sem=c_ssem.at[k], recv_sem=c_rsem.at[q],
            device_id=(s, q), device_id_type=MESH).wait_recv()

    @pl.when(has_right)
    def _():
        cur_copy(cur_right, cr_ssem.at[0], cr_rsem, (s, p)).wait_recv()

    @pl.when(has_left)
    def _():
        cur_copy(cur_left, cl_ssem.at[0], cl_rsem, (s, p)).wait_recv()

    tiles = []
    for tile in range(L // TILE):
        value = cur_peers[tile * per_tile]
        for b in range(1, per_tile):
            value = jnp.where(lane_t < b * width, value, cur_peers[tile * per_tile + b])
        tiles.append(value)
    beyond = jnp.where(lane_t < TILE // 2, cur_right[...], cur_left[...])
    current = jnp.concatenate(tiles + [beyond], axis=1)
    current = jnp.where(row16 < K, current, 0.0)
    relax = jnp.concatenate([relax, beyond[K:K + 1]], axis=1)

    def own_shift(x):
        return jnp.where(positive, roll(x, 1), roll(x, -1))

    alpha = 1.0 - c_vx - relax
    weights = [jnp.ones((nvx, W), f32)] + [jnp.zeros((nvx, W), f32)] * ITERS
    for n in range(ITERS):
        shifted = [own_shift(a) for a in weights[:-1]]
        weights = [alpha * weights[0]] + [
            alpha * weights[i] + c_vx * shifted[i - 1] for i in range(1, ITERS + 1)]
    for i in range(ITERS + 1):
        coef_ref[i] = weights[i][:, :L]
    for j in range(nvx):
        m = j % members
        t = row8 - 4 * m
        value = jnp.zeros((8, L), f32)
        for i in range(1, ITERS + 1):
            near = jnp.where(positive, col8, L - 1 - col8)
            value = jnp.where((near + 1 + t == i) & (t >= 0) & (t < ITERS), weights[i][j:j + 1, :L], value)
        high, low = split(value)
        zc_ref[j, 32:48, :] = jnp.concatenate([high.astype(f32), low.astype(f32)], axis=0).astype(jnp.bfloat16)

    for g in range(group):
        for k in range(1, N):
            q = lax.rem(p + k, N)
            rows = pl.ds(pl.multiple_of(q * R + g * members * Q, 8), members * Q)
            pltpu.make_async_remote_copy(
                src_ref=g_all.at[rows, pl.ds(0, L)], dst_ref=g_all.at[rows, pl.ds(0, L)],
                send_sem=g_ssem.at[g, k], recv_sem=g_rsem.at[g, q],
                device_id=(s, q), device_id_type=MESH).wait_recv()

    def pack_wait(dst, ssem, rsem):
        for q in range(N):
            pltpu.make_async_remote_copy(
                src_ref=pack_l, dst_ref=dst.at[q], send_sem=ssem.at[q], recv_sem=rsem.at[q],
                device_id=(s, q), device_id_type=MESH).wait_recv()

    @pl.when(has_right)
    def _():
        pack_wait(from_right, pl_ssem, pl_rsem)

    @pl.when(has_left)
    def _():
        pack_wait(from_left, pr_ssem, pr_rsem)

    for q in range(N):
        right = from_right[q]
        left = from_left[q]
        for j in range(nvx):
            value = jnp.where(lane8 < TILE // 2, roll(right, -HALO * j), roll(left, TILE - HALO - HALO * j))
            g_all[q * R + j * Q:q * R + (j + 1) * Q, L:W] = value

    half = NV1 * Q // 2

    def all_shift(x):
        return jnp.concatenate([roll(x[:half], -1), roll(x[half:], 1)], axis=0)

    def operator(r):
        applied = jnp.dot(coupling, r, precision=lax.Precision.HIGHEST, preferred_element_type=f32)
        applied = applied + diffusion * (2.0 * r - roll(r, 1) - roll(r, -1))
        return jnp.where(inside, applied, 0.0)

    def own_sum(x):
        total = x[:, 0:TILE]
        for tile in range(1, L // TILE):
            total = total + x[:, tile * TILE:(tile + 1) * TILE]
        return jnp.sum(total, axis=0, keepdims=True)

    keep_all = 1.0 - c_all - relax
    keep_own = 1.0 - c_own - relax
    beta_own = beta_ref[pl.ds(pl.multiple_of(p * R, 16), R), :]
    state = g_all[...]
    source = None

    def sum_copy(n, t):
        target = lax.rem(s + t, S)
        return pltpu.make_async_remote_copy(
            src_ref=sums.at[n, s], dst_ref=sums.at[n, s], send_sem=s_ssem.at[n, t], recv_sem=s_rsem.at[n, s],
            device_id=(target, p), device_id_type=MESH)

    for n in range(ITERS):
        moved = keep_all * state + c_all * all_shift(state)
        pull = scale * relax * current
        high, low = split(moved)
        twice = dot(moments_ref[...], high)
        shares = twice[:16] + twice[16:] + dot(moments_ref[0:16, :], low) + dot_parts(inner_ref[...], pull)
        shares = jnp.where(inside, shares, 0.0)
        r = shares - current
        a1 = operator(r)
        a2 = operator(a1)
        sums[n, s] = jnp.concatenate(
            [own_sum(r * r), own_sum(r * a1), own_sum(a1 * a1), own_sum(a1 * a2), jnp.zeros((4, TILE), f32)], axis=0)
        for t in range(1, S):
            sum_copy(n, t).start()
        for t in range(1, S):
            q = lax.rem(s + t, S)
            pltpu.make_async_remote_copy(
                src_ref=sums.at[n, q], dst_ref=sums.at[n, q], send_sem=s_ssem.at[n, t], recv_sem=s_rsem.at[n, q],
                device_id=(q, p), device_id_type=MESH).wait_recv()
        total = sums[n, 0]
        for t in range(1, S):
            total = total + sums[n, t]
        total = jnp.sum(total, axis=1, keepdims=True)
        m0, m1, m2, m3 = (total[i:i + 1] for i in range(4))
        first = m0 / m1
        second = (m0 - 2.0 * first * m1 + first * first * m2) / (m1 - 2.0 * first * m2 + first * first * m3)
        correction = first * r + second * (r - first * a1)
        current = shares + correction
        z = pull + correction
        if n < ITERS - 1:
            state = moved + dot_parts(project_ref[...], z)
        fresh = dot_parts(beta_own, z)
        source = fresh if source is None else keep_own * source + c_own * own_shift(source) + fresh

    for j in range(nvx):
        high, low = split(source[j * Q:(j + 1) * Q, :L])
        pair = jnp.concatenate([high.astype(f32), low.astype(f32)], axis=0).astype(jnp.bfloat16)
        zc_ref[j, 0:16, :] = pair
        zc_ref[j, 16:32, :] = pair

    chosen = current[:, 0:TILE]
    for tile in range(1, L // TILE):
        chosen = jnp.where(p >= tile * per_tile, current[:, tile * TILE:(tile + 1) * TILE], chosen)
    place = lax.rem(p, per_tile)
    for b in range(per_tile):
        @pl.when(place == b)
        def _():
            out_ref[...] = chosen[:K, b * width:(b + 1) * width]

    @pl.when(has_up)
    def _():
        for g in range(group):
            edge_copy(g, s).wait_recv()

    halo_ref[...] = edge_recv[...]

    for k in range(1, N):
        cur_copy(cur_peers.at[p], c_ssem.at[k], c_rsem.at[p], (s, lax.rem(p + k, N))).wait_send()
        for g in range(group):
            g_copy(g, k).wait_send()

    @pl.when((p == 0) & has_left)
    def _():
        for q in range(N):
            cur_copy(cur_right, cr_ssem.at[q], cr_rsem, (s - 1, q)).wait_send()

    @pl.when((p == N - 1) & has_right)
    def _():
        for q in range(N):
            cur_copy(cur_left, cl_ssem.at[q], cl_rsem, (s + 1, q)).wait_send()

    @pl.when(has_down)
    def _():
        for g in range(group):
            edge_copy(g, downwind).wait_send()

    @pl.when(has_left)
    def _():
        for q in range(N):
            pack_copy(pack_l, from_right, pl_ssem.at[q], pl_rsem, (s - 1, q)).wait_send()

    @pl.when(has_right)
    def _():
        for q in range(N):
            pack_copy(pack_r, from_left, pr_ssem.at[q], pr_rsem, (s + 1, q)).wait_send()

    for n in range(ITERS):
        for t in range(1, S):
            sum_copy(n, t).wait_send()


def result_kernel(N, members, h_ref, zc_ref, coef_ref, halo_ref, phi_ref, out_ref):
    j = pl.program_id(0)
    L = h_ref.shape[1]
    positive = lax.axis_index("vel") >= N // 2
    row = lax.broadcasted_iota(jnp.int32, (L, L), 0)
    col = lax.broadcasted_iota(jnp.int32, (L, L), 1)
    distance = jnp.where(positive, col - row, row - col)
    band = jnp.zeros((L, L), jnp.float32)
    for i in range(ITERS + 1):
        band = jnp.where(distance == i, coef_ref[i, pl.ds(j, 1), :], band)
    high, low = split(band)
    block = h_ref[...]
    edge = halo_ref[j // members]
    rows = jnp.concatenate([phi_ref[...], jnp.concatenate([edge, edge], axis=0).astype(jnp.bfloat16)], axis=0)
    total = dot(block, high) + dot(block, low)
    total = total + lax.dot_general(
        rows, zc_ref[0], (((0,), (0,)), ((), ())), preferred_element_type=jnp.float32)
    out_ref[...] = total.astype(jnp.bfloat16)


def solution(mesh):
    S, N = mesh.shape["space"], mesh.shape["vel"]
    table = tables()
    plane = NV1 * NV1

    def per_device(velocity_dist, macro_state, collision_rate, wall_flags, diffusivity, coupling):
        V, L = velocity_dist.shape
        width = macro_state.shape[1]
        nvx = V // plane
        members = 2
        group = nvx // members
        assert N % 2 == 0 and nvx % 2 == 0 and HALO * nvx <= TILE and width >= HALO and TILE % width == 0
        f32, bf16 = jnp.float32, jnp.bfloat16
        vmem = pl.BlockSpec(memory_space=pltpu.VMEM)
        smem = pl.BlockSpec(memory_space=pltpu.SMEM)
        dma = pltpu.SemaphoreType.DMA
        zc, coef, halo, macro = pl.pallas_call(
            lambda *refs: moments_kernel(S, N, *refs),
            out_shape=(
                jax.ShapeDtypeStruct((nvx, 48, L), bf16),
                jax.ShapeDtypeStruct((ITERS + 1, nvx, L), f32),
                jax.ShapeDtypeStruct((group, 8, plane), f32),
                jax.ShapeDtypeStruct(macro_state.shape, f32),
            ),
            in_specs=[pl.BlockSpec(memory_space=pl.ANY), vmem, vmem, vmem, smem, vmem] + [vmem] * 5,
            out_specs=(vmem,) * 4,
            scratch_shapes=[
                pltpu.VMEM((V, L), bf16),
                pltpu.VMEM((NV1 * Q, L + TILE), f32),
                pltpu.VMEM((16, TILE), f32),
                pltpu.VMEM((N, 16, TILE), f32),
                pltpu.VMEM((16, TILE), f32),
                pltpu.VMEM((16, TILE), f32),
                pltpu.VMEM((8, TILE), f32),
                pltpu.VMEM((8, TILE), f32),
                pltpu.VMEM((N, 8, TILE), f32),
                pltpu.VMEM((N, 8, TILE), f32),
                pltpu.VMEM((group, 8, plane), f32),
                pltpu.VMEM((group, 8, plane), f32),
                pltpu.VMEM((ITERS, S, 8, TILE), f32),
                pltpu.VMEM((16, 16), f32),
                dma((nvx,)), dma((group, N)), dma((group, N)),
                dma((N,)), dma((N,)), dma((N,)), dma(()), dma((N,)), dma(()),
                dma((N,)), dma((N,)), dma((N,)), dma((N,)),
                dma((group,)), dma((group,)), dma((ITERS, S)), dma((ITERS, S)),
            ],
            compiler_params=pltpu.CompilerParams(
                collective_id=0, has_side_effects=True, vmem_limit_bytes=40 * 1024 * 1024),
        )(
            velocity_dist, macro_state, collision_rate[None, :], wall_flags[None, :], diffusivity, coupling,
            *(jnp.asarray(table[name]) for name in ("reduce", "project", "beta", "moments", "inner")),
        )
        dist = pl.pallas_call(
            lambda *refs: result_kernel(N, members, *refs),
            grid=(nvx,),
            out_shape=jax.ShapeDtypeStruct((V, L), bf16),
            in_specs=[
                pl.BlockSpec((plane, L), lambda j: (j, 0)),
                pl.BlockSpec((1, 48, L), lambda j: (j, 0, 0)),
                vmem, vmem, vmem,
            ],
            out_specs=pl.BlockSpec((plane, L), lambda j: (j, 0)),
            compiler_params=pltpu.CompilerParams(vmem_limit_bytes=40 * 1024 * 1024),
        )(velocity_dist, zc, coef, halo, jnp.asarray(table["phi"]))
        return dist, macro

    placed = (P("vel", "space"), P(None, ("space", "vel")), P("space"), P("space"), P(), P())
    return jax.shard_map(
        per_device,
        mesh=mesh,
        in_specs=placed,
        out_specs=(P("vel", "space"), P(None, ("space", "vel"))),
        check_vma=False,
    )
```

```python
import math

import jax
import jax.numpy as jnp
import numpy as np
from jax import lax
from jax.experimental import pallas as pl
from jax.experimental.pallas import tpu as pltpu
from jax.sharding import PartitionSpec as P

NV1 = 32
ITERS = 3
SWEEPS = 2
K = 13
Q = 8
HALO = 8
TILE = 128
GRANT = 60 * 1024 * 1024
MESH = pl.DeviceIdType.MESH

speed_limit = 4.0
time_step = 0.125
shakhov_weights = (1.0,) * 5 + (0.0,) * 5 + (1.0 / 3.0,) * 3


def two_parts(x):
    high = np.asarray(x, np.float32).astype(jnp.bfloat16)
    low = (np.asarray(x, np.float32) - high.astype(np.float32)).astype(jnp.bfloat16)
    return high, low


def tables():
    spacing = 2.0 * speed_limit / NV1
    v = (np.arange(NV1) + 0.5) * spacing - speed_limit
    w1 = np.exp(-0.5 * v * v) * spacing / math.sqrt(2.0 * math.pi)
    y = np.repeat(v, NV1)
    z = np.tile(v, NV1)
    w_yz = np.repeat(w1, NV1) * np.tile(w1, NV1)
    phi = np.stack([np.ones_like(y), y, z, y * y, z * z, y * z, y * (y * y + z * z), z * (y * y + z * z)])
    beta = np.zeros((NV1, Q, 16))
    r6, r12, r10 = math.sqrt(6.0), math.sqrt(12.0), math.sqrt(10.0)
    beta[:, 0, 0] = 1.0
    beta[:, 0, 1] = v
    beta[:, 1, 2] = 1.0
    beta[:, 2, 3] = 1.0
    beta[:, 0, 4], beta[:, 3, 4], beta[:, 4, 4] = (v * v - 3.0) / r6, 1.0 / r6, 1.0 / r6
    beta[:, 1, 5] = v
    beta[:, 2, 6] = v
    beta[:, 5, 7] = 1.0
    beta[:, 0, 8], beta[:, 3, 8] = 0.5 * v * v, -0.5
    beta[:, 0, 9], beta[:, 3, 9], beta[:, 4, 9] = v * v / r12, 1.0 / r12, -2.0 / r12
    beta[:, 0, 10], beta[:, 3, 10], beta[:, 4, 10] = v * (v * v - 5.0) / r10, v / r10, v / r10
    beta[:, 1, 11], beta[:, 6, 11] = (v * v - 5.0) / r10, 1.0 / r10
    beta[:, 2, 12], beta[:, 7, 12] = (v * v - 5.0) / r10, 1.0 / r10
    gram = (phi * w_yz) @ phi.T
    rows = NV1 * Q
    project = np.einsum("qr,vrk->vqk", gram, beta).reshape(rows, 16)
    moments = (w1[:, None, None] * beta).reshape(rows, 16).T
    inner = moments @ project
    c = np.repeat(time_step * np.abs(v), Q)
    half = rows // 2
    step = np.concatenate(
        [
            (moments * (1.0 - c)) @ project,
            (moments * c)[:, half:] @ project[half:],
            (moments * c)[:, :half] @ project[:half],
            inner,
        ],
        axis=1,
    )

    def left(a):
        high, low = two_parts(a)
        return np.concatenate([high, high, low], axis=1)

    reduce_h, reduce_l = two_parts(phi * w_yz)
    phi_h, phi_l = two_parts(phi)
    m_h, m_l = two_parts(moments)
    return dict(
        reduce=np.concatenate([reduce_h, reduce_l]),
        phi=np.concatenate([phi_h, phi_h, phi_l, phi_l]),
        project=left(project),
        beta=left(beta.reshape(rows, 16)),
        moments=np.concatenate([m_h, m_l]),
        inner=left(inner),
        step=left(step),
    )


def split(x):
    high = x.astype(jnp.bfloat16)
    return high, (x - high.astype(jnp.float32)).astype(jnp.bfloat16)


def dot(a, b):
    return jnp.dot(a, b, preferred_element_type=jnp.float32)


def dot_parts(left, x):
    high, low = split(x)
    return dot(left, jnp.concatenate([high, low, high], axis=0))


def roll(x, shift):
    return pltpu.roll(x, shift % x.shape[1], 1)


def moments_kernel(
    S, N,
    h_ref, *refs,
):
    count = 11
    sources = refs[:count]
    band_hbm, zc_ref, halo_ref, out_ref = refs[count:count + 4]
    buffers = refs[count + 4:2 * count + 4]
    (
    h_buf, band_ref, g_all, cur_stage, cur_peers, cur_left, cur_right,
    pack_l, pack_r, from_left, from_right, edge_send, edge_recv, sums, coup_pad, diag_pad,
    small_sem, band_sem, h_sem, g_ssem, g_rsem, c_ssem, c_rsem, cl_ssem, cl_rsem, cr_ssem, cr_rsem,
    pl_ssem, pl_rsem, pr_ssem, pr_rsem, e_ssem, e_rsem, s_ssem, s_rsem,
    ) = refs[2 * count + 4:]
    (macro_ref, rate_ref, wall_ref, reduce_ref, diff_ref, coup_ref,
     project_ref, beta_ref, moments_ref, inner_ref, step_ref) = buffers
    L = h_ref.shape[1]
    W = L + TILE
    width = macro_ref.shape[1]
    per_tile = TILE // width
    plane = NV1 * NV1
    nvx = h_ref.shape[0] // plane
    R = nvx * Q
    group = edge_send.shape[0]
    members = nvx // group
    s = lax.axis_index("space")
    p = lax.axis_index("vel")
    positive = p >= N // 2
    has_left = s > 0
    has_right = s < S - 1
    f32 = jnp.float32

    def small(i):
        return pltpu.make_async_copy(sources[i], buffers[i], small_sem.at[i])

    for i in range(4):
        small(i).start()
    for j in range(nvx):
        pltpu.make_async_copy(h_ref.at[pl.ds(j * plane, plane)], h_buf.at[pl.ds(j * plane, plane)], h_sem.at[j]).start()

    for i in range(4, count):
        small(i).start()

    cur_left[...] = jnp.zeros_like(cur_left)
    cur_right[...] = jnp.zeros_like(cur_right)
    from_left[...] = jnp.zeros_like(from_left)
    from_right[...] = jnp.zeros_like(from_right)
    edge_recv[...] = jnp.zeros_like(edge_recv)

    barrier = pltpu.get_barrier_semaphore()

    def greet(device):
        pl.semaphore_signal(barrier, inc=1, device_id=device, device_id_type=MESH)

    for k in range(1, N):
        greet((s, lax.rem(p + k, N)))

    @pl.when(has_left)
    def _():
        for q in range(N):
            greet((s - 1, q))

    @pl.when(has_right)
    def _():
        for q in range(N):
            greet((s + 1, q))

    for t in range(S):
        @pl.when((t != s) & (t != s - 1) & (t != s + 1))
        def _():
            greet((t, p))

    beside = has_left.astype(jnp.int32) + has_right.astype(jnp.int32)
    greetings = (N - 1) + N * beside + (S - 1 - beside)

    for i in range(4):
        small(i).wait()

    relax = time_step * rate_ref[...] * (1.0 + wall_ref[...].astype(f32))
    edge_relax = jnp.where(p == 0, relax[:, :TILE], relax[:, L - TILE:])
    cur_stage[...] = jnp.zeros_like(cur_stage)
    cur_stage[0:K, :] = jnp.concatenate([macro_ref[...]] * per_tile, axis=1)
    cur_stage[K:K + 1, :] = edge_relax
    cur_peers[p] = cur_stage[...]

    coup_pad[...] = jnp.zeros_like(coup_pad)
    diag_pad[...] = jnp.zeros_like(diag_pad)

    row8 = lax.broadcasted_iota(jnp.int32, (8, L), 0)
    col8 = lax.broadcasted_iota(jnp.int32, (8, L), 1)
    near = jnp.where(positive, col8, L - 1 - col8)
    row_p = lax.broadcasted_iota(jnp.int32, (8, members * TILE), 0)
    col_p = lax.broadcasted_iota(jnp.int32, (8, members * TILE), 1)
    t_p = row_p % 4
    picked = (row_p // 4 == col_p // TILE) & (t_p == jnp.where(positive, TILE - 1 - col_p % TILE, col_p % TILE))
    pick = (picked & (t_p < ITERS)).astype(f32).astype(jnp.bfloat16)
    edge_lanes = pl.ds(pl.multiple_of(jnp.where(positive, L - TILE, 0), TILE), TILE)

    reduce = reduce_ref[...]
    lane8 = lax.broadcasted_iota(jnp.int32, (8, TILE), 1)
    packed_l = jnp.zeros((8, TILE), f32)
    packed_r = jnp.zeros((8, TILE), f32)

    def cur_copy(dst, ssem, rsem, device):
        return pltpu.make_async_remote_copy(
            src_ref=cur_stage, dst_ref=dst, send_sem=ssem, recv_sem=rsem, device_id=device, device_id_type=MESH)

    def g_copy(g, k):
        rows = pl.ds(pl.multiple_of(p * R + g * members * Q, 8), members * Q)
        return pltpu.make_async_remote_copy(
            src_ref=g_all.at[rows, pl.ds(0, L)], dst_ref=g_all.at[rows, pl.ds(0, L)],
            send_sem=g_ssem.at[g, k], recv_sem=g_rsem.at[g, p],
            device_id=(s, lax.rem(p + k, N)), device_id_type=MESH)

    def edge_copy(g, target):
        return pltpu.make_async_remote_copy(
            src_ref=edge_send.at[g], dst_ref=edge_recv.at[g],
            send_sem=e_ssem.at[g], recv_sem=e_rsem.at[g],
            device_id=(target, p), device_id_type=MESH)

    downwind = jnp.where(positive, s + 1, s - 1)
    has_down = (downwind >= 0) & (downwind < S)
    has_up = jnp.where(positive, s - 1, S - 2 - s) >= 0

    for g in range(group):
        for m in range(members):
            j = g * members + m
            pltpu.make_async_copy(
                h_ref.at[pl.ds(j * plane, plane)], h_buf.at[pl.ds(j * plane, plane)], h_sem.at[j]).wait()
            block = h_buf[j * plane:(j + 1) * plane, :]
            both = dot(reduce, block)
            value = both[:Q] + both[Q:]
            g_all[pl.ds(pl.multiple_of(p * R + j * Q, 8), Q), 0:L] = value
            here = (lane8 >= HALO * j) & (lane8 < HALO * (j + 1))
            packed_l = jnp.where(here, roll(value[:, :TILE], HALO * j), packed_l)
            packed_r = jnp.where(here, roll(value[:, L - TILE:], HALO * j - (TILE - HALO)), packed_r)
        if g == 0:
            pl.semaphore_wait(barrier, greetings)
            for k in range(1, N):
                cur_copy(cur_peers.at[p], c_ssem.at[k], c_rsem.at[p], (s, lax.rem(p + k, N))).start()

            @pl.when((p == 0) & has_left)
            def _():
                for q in range(N):
                    cur_copy(cur_right, cr_ssem.at[q], cr_rsem, (s - 1, q)).start()

            @pl.when((p == N - 1) & has_right)
            def _():
                for q in range(N):
                    cur_copy(cur_left, cl_ssem.at[q], cl_rsem, (s + 1, q)).start()

        for k in range(1, N):
            g_copy(g, k).start()

    pack_l[...] = packed_l
    pack_r[...] = packed_r

    def pack_copy(src, dst, ssem, rsem, device):
        return pltpu.make_async_remote_copy(
            src_ref=src, dst_ref=dst.at[p], send_sem=ssem, recv_sem=rsem.at[p], device_id=device, device_id_type=MESH)

    @pl.when(has_left)
    def _():
        for q in range(N):
            pack_copy(pack_l, from_right, pl_ssem.at[q], pl_rsem, (s - 1, q)).start()

    @pl.when(has_right)
    def _():
        for q in range(N):
            pack_copy(pack_r, from_left, pr_ssem.at[q], pr_rsem, (s + 1, q)).start()

    for g in range(group):
        block = jnp.concatenate(
            [h_buf[j * plane:(j + 1) * plane, edge_lanes] for j in range(g * members, (g + 1) * members)], axis=1)
        edge_send[g] = lax.dot_general(pick, block, (((1,), (1,)), ((), ())), preferred_element_type=f32)

        @pl.when(has_down)
        def _():
            edge_copy(g, downwind).start()

    for i in range(4, count):
        small(i).wait()
    coup_pad[0:K, 0:K] = coup_ref[...]
    eye = lax.broadcasted_iota(jnp.int32, (K, K), 0) == lax.broadcasted_iota(jnp.int32, (K, K), 1)
    diag_pad[0:K, 0:K] = jnp.where(eye, jnp.broadcast_to(diff_ref[...], (K, K)), 0.0)
    diffusion = jnp.sum(diag_pad[...], axis=1, keepdims=True)
    vx_row = lax.broadcasted_iota(jnp.int32, (NV1 * Q, 1), 0) // Q
    c_all = time_step * jnp.abs((vx_row.astype(f32) + 0.5) * (2.0 * speed_limit / NV1) - speed_limit)
    own_row = lax.broadcasted_iota(jnp.int32, (R, 1), 0) // Q + p * nvx
    c_own = time_step * jnp.abs((own_row.astype(f32) + 0.5) * (2.0 * speed_limit / NV1) - speed_limit)
    own_vx = lax.broadcasted_iota(jnp.int32, (nvx, 1), 0) + p * nvx
    c_vx = time_step * jnp.abs((own_vx.astype(f32) + 0.5) * (2.0 * speed_limit / NV1) - speed_limit)
    row16 = lax.broadcasted_iota(jnp.int32, (16, 1), 0)
    scale = jnp.zeros((16, 1), f32)
    for k in range(K):
        scale = jnp.where(row16 == k, shakhov_weights[k], scale)
    lane = lax.broadcasted_iota(jnp.int32, (1, W), 1)
    cell = jnp.where(lane < L + TILE // 2, lane, lane - W) + s * L
    inside = (cell >= 0) & (cell < S * L)
    lane_t = lax.broadcasted_iota(jnp.int32, (1, TILE), 1)
    coupling = coup_pad[...]

    for k in range(1, N):
        q = lax.rem(p + k, N)
        pltpu.make_async_remote_copy(
            src_ref=cur_stage, dst_ref=cur_peers.at[q], send_sem=c_ssem.at[k], recv_sem=c_rsem.at[q],
            device_id=(s, q), device_id_type=MESH).wait_recv()

    @pl.when(has_right)
    def _():
        cur_copy(cur_right, cr_ssem.at[0], cr_rsem, (s, p)).wait_recv()

    @pl.when(has_left)
    def _():
        cur_copy(cur_left, cl_ssem.at[0], cl_rsem, (s, p)).wait_recv()

    tiles = []
    for tile in range(L // TILE):
        value = cur_peers[tile * per_tile]
        for b in range(1, per_tile):
            value = jnp.where(lane_t < b * width, value, cur_peers[tile * per_tile + b])
        tiles.append(value)
    beyond = jnp.where(lane_t < TILE // 2, cur_right[...], cur_left[...])
    current = jnp.concatenate(tiles + [beyond], axis=1)
    current = jnp.where(row16 < K, current, 0.0)
    relax = jnp.concatenate([relax, beyond[K:K + 1]], axis=1)

    def own_shift(x):
        return jnp.where(positive, roll(x, 1), roll(x, -1))

    alpha = 1.0 - c_vx - relax
    weights = [jnp.ones((nvx, W), f32)] + [jnp.zeros((nvx, W), f32)] * ITERS
    for n in range(ITERS):
        shifted = [own_shift(a) for a in weights[:-1]]
        weights = [alpha * weights[0]] + [
            alpha * weights[i] + c_vx * shifted[i - 1] for i in range(1, ITERS + 1)]
    def band_copy(j):
        return pltpu.make_async_copy(band_ref.at[j], band_hbm.at[j], band_sem.at[j])

    def bands(j):
        row = lax.broadcasted_iota(jnp.int32, (L, L), 0)
        col = lax.broadcasted_iota(jnp.int32, (L, L), 1)
        distance = jnp.where(positive, col - row, row - col)
        band = jnp.zeros((L, L), f32)
        t = row8 - 4 * (j % members)
        value = jnp.zeros((8, L), f32)
        for i in range(ITERS + 1):
            line = weights[i][j:j + 1, :L]
            band = jnp.where(distance == i, line, band)
            value = jnp.where((near + 1 + t == i) & (t >= 0) & (t < ITERS), line, value)
        band_ref[j, 0:L, :], band_ref[j, L:2 * L, :] = split(band)
        band_copy(j).start()
        high, low = split(value)
        zc_ref[j, 32:48, :] = jnp.concatenate([high.astype(f32), low.astype(f32)], axis=0).astype(jnp.bfloat16)

    for g in range(group):
        for k in range(1, N):
            q = lax.rem(p + k, N)
            rows = pl.ds(pl.multiple_of(q * R + g * members * Q, 8), members * Q)
            pltpu.make_async_remote_copy(
                src_ref=g_all.at[rows, pl.ds(0, L)], dst_ref=g_all.at[rows, pl.ds(0, L)],
                send_sem=g_ssem.at[g, k], recv_sem=g_rsem.at[g, q],
                device_id=(s, q), device_id_type=MESH).wait_recv()

    def pack_wait(dst, ssem, rsem):
        for q in range(N):
            pltpu.make_async_remote_copy(
                src_ref=pack_l, dst_ref=dst.at[q], send_sem=ssem.at[q], recv_sem=rsem.at[q],
                device_id=(s, q), device_id_type=MESH).wait_recv()

    @pl.when(has_right)
    def _():
        pack_wait(from_right, pl_ssem, pl_rsem)

    @pl.when(has_left)
    def _():
        pack_wait(from_left, pr_ssem, pr_rsem)

    for q in range(N):
        right = from_right[q]
        left = from_left[q]
        for j in range(nvx):
            value = jnp.where(lane8 < TILE // 2, roll(right, -HALO * j), roll(left, TILE - HALO - HALO * j))
            g_all[q * R + j * Q:q * R + (j + 1) * Q, L:W] = value

    half = NV1 * Q // 2

    def all_shift(x):
        return jnp.concatenate([roll(x[:half], -1), roll(x[half:], 1)], axis=0)

    def operator(r):
        applied = diffusion * (2.0 * r - roll(r, 1) - roll(r, -1))
        for k in range(K):
            applied = applied + coupling[:, k:k + 1] * r[k:k + 1, :]
        return jnp.where(inside, applied, 0.0)

    def own_sum(x):
        total = x[:, 0:TILE]
        for tile in range(1, L // TILE):
            total = total + x[:, tile * TILE:(tile + 1) * TILE]
        return jnp.sum(total, axis=0, keepdims=True)

    keep_all = 1.0 - c_all - relax
    keep_own = 1.0 - c_own - relax
    beta_own = beta_ref[pl.ds(pl.multiple_of(p * R, 16), R), :]
    state = g_all[...]
    source = None

    def sum_copy(n, t):
        target = lax.rem(s + t, S)
        return pltpu.make_async_remote_copy(
            src_ref=sums.at[n, s], dst_ref=sums.at[n, s], send_sem=s_ssem.at[n, t], recv_sem=s_rsem.at[n, s],
            device_id=(target, p), device_id_type=MESH)

    def transport(x):
        return keep_all * x + c_all * all_shift(x)

    def moments_of(x):
        high, low = split(x)
        twice = dot(moments_ref[...], high)
        return twice[:16] + twice[16:] + dot(moments_ref[0:16, :], low)

    moved = transport(state)
    base = moments_of(moved)
    z = None
    for n in range(ITERS):
        pull = scale * relax * current
        if n == 0:
            shares = base + dot_parts(inner_ref[...], pull)
        else:
            shares = base + dot_parts(
                step_ref[...], jnp.concatenate([z, roll(z, 1), roll(z, -1), pull - relax * z], axis=0))
        shares = jnp.where(inside, shares, 0.0)
        r = shares - current
        a1 = operator(r)
        a2 = operator(a1)
        sums[n, s] = jnp.concatenate(
            [own_sum(r * r), own_sum(r * a1), own_sum(a1 * a1), own_sum(a1 * a2), jnp.zeros((4, TILE), f32)], axis=0)
        for t in range(1, S):
            sum_copy(n, t).start()
        if n > 0:
            fresh = dot_parts(beta_own, z)
            source = fresh if source is None else drift + fresh
            drift = keep_own * source + c_own * own_shift(source)
        if n < ITERS - 1:
            if n > 0:
                moved = transport(moved + dot_parts(project_ref[...], z))
            base = moments_of(transport(moved))
        for j in range(n * nvx // ITERS, (n + 1) * nvx // ITERS):
            bands(j)
        for t in range(1, S):
            q = lax.rem(s + t, S)
            pltpu.make_async_remote_copy(
                src_ref=sums.at[n, q], dst_ref=sums.at[n, q], send_sem=s_ssem.at[n, t], recv_sem=s_rsem.at[n, q],
                device_id=(q, p), device_id_type=MESH).wait_recv()
        total = sums[n, 0]
        for t in range(1, S):
            total = total + sums[n, t]
        total = jnp.sum(total, axis=1, keepdims=True)
        m0, m1, m2, m3 = (total[i:i + 1] for i in range(4))
        first = m0 / m1
        second = (m0 - 2.0 * first * m1 + first * first * m2) / (m1 - 2.0 * first * m2 + first * first * m3)
        correction = first * r + second * (r - first * a1)
        current = shares + correction
        z = pull + correction
    source = drift + dot_parts(beta_own, z)

    for j in range(nvx):
        high, low = split(source[j * Q:(j + 1) * Q, :L])
        pair = jnp.concatenate([high.astype(f32), low.astype(f32)], axis=0).astype(jnp.bfloat16)
        zc_ref[j, 0:16, :] = pair
        zc_ref[j, 16:32, :] = pair

    chosen = current[:, 0:TILE]
    for tile in range(1, L // TILE):
        chosen = jnp.where(p >= tile * per_tile, current[:, tile * TILE:(tile + 1) * TILE], chosen)
    place = lax.rem(p, per_tile)
    for b in range(per_tile):
        @pl.when(place == b)
        def _():
            out_ref[...] = chosen[:K, b * width:(b + 1) * width]

    @pl.when(has_up)
    def _():
        for g in range(group):
            edge_copy(g, s).wait_recv()

    for g in range(group):
        halo_ref[g] = jnp.concatenate([edge_recv[g], edge_recv[g]], axis=0).astype(jnp.bfloat16)

    for j in range(nvx):
        band_copy(j).wait()

    for k in range(1, N):
        cur_copy(cur_peers.at[p], c_ssem.at[k], c_rsem.at[p], (s, lax.rem(p + k, N))).wait_send()
        for g in range(group):
            g_copy(g, k).wait_send()

    @pl.when((p == 0) & has_left)
    def _():
        for q in range(N):
            cur_copy(cur_right, cr_ssem.at[q], cr_rsem, (s - 1, q)).wait_send()

    @pl.when((p == N - 1) & has_right)
    def _():
        for q in range(N):
            cur_copy(cur_left, cl_ssem.at[q], cl_rsem, (s + 1, q)).wait_send()

    @pl.when(has_down)
    def _():
        for g in range(group):
            edge_copy(g, downwind).wait_send()

    @pl.when(has_left)
    def _():
        for q in range(N):
            pack_copy(pack_l, from_right, pl_ssem.at[q], pl_rsem, (s - 1, q)).wait_send()

    @pl.when(has_right)
    def _():
        for q in range(N):
            pack_copy(pack_r, from_left, pr_ssem.at[q], pr_rsem, (s + 1, q)).wait_send()

    for n in range(ITERS):
        for t in range(1, S):
            sum_copy(n, t).wait_send()


def result_kernel(members, h_ref, band_ref, zc_ref, halo_ref, macro_ref, phi_ref, out_ref, macro_out_ref):
    j = pl.program_id(0)
    L = h_ref.shape[1]

    @pl.when(j == 0)
    def _():
        macro_out_ref[...] = macro_ref[...]

    block = h_ref[...]
    rows = jnp.concatenate([phi_ref[...], halo_ref[j // members]], axis=0)
    total = dot(block, band_ref[0, 0:L, :]) + dot(block, band_ref[0, L:2 * L, :])
    total = total + lax.dot_general(
        rows, zc_ref[0], (((0,), (0,)), ((), ())), preferred_element_type=jnp.float32)
    out_ref[...] = total.astype(jnp.bfloat16)


def solution(mesh):
    S, N = mesh.shape["space"], mesh.shape["vel"]
    table = tables()
    plane = NV1 * NV1

    def per_device(velocity_dist, macro_state, collision_rate, wall_flags, diffusivity, coupling):
        V, L = velocity_dist.shape
        width = macro_state.shape[1]
        nvx = V // plane
        members = 2
        group = nvx // members
        assert N % 2 == 0 and nvx % 2 == 0 and HALO * nvx <= TILE and width >= HALO and TILE % width == 0
        f32, bf16 = jnp.float32, jnp.bfloat16
        vmem = pl.BlockSpec(memory_space=pltpu.VMEM)
        hbm = pl.BlockSpec(memory_space=pltpu.HBM)
        dma = pltpu.SemaphoreType.DMA
        small = [
            macro_state, collision_rate[None, :], wall_flags[None, :], jnp.asarray(table["reduce"]),
            diffusivity[None, :], coupling,
        ] + [jnp.asarray(table[name]) for name in ("project", "beta", "moments", "inner", "step")]
        band, zc, halo, macro = pl.pallas_call(
            lambda *refs: moments_kernel(S, N, *refs),
            out_shape=(
                jax.ShapeDtypeStruct((nvx, 2 * L, L), bf16),
                jax.ShapeDtypeStruct((nvx, 48, L), bf16),
                jax.ShapeDtypeStruct((group, 16, plane), bf16),
                jax.ShapeDtypeStruct(macro_state.shape, f32),
            ),
            in_specs=[hbm] * (1 + len(small)),
            out_specs=(hbm,) + (vmem,) * 3,
            scratch_shapes=[
                *(pltpu.VMEM(x.shape, x.dtype) for x in small),
                pltpu.VMEM((V, L), bf16),
                pltpu.VMEM((nvx, 2 * L, L), bf16),
                pltpu.VMEM((NV1 * Q, L + TILE), f32),
                pltpu.VMEM((16, TILE), f32),
                pltpu.VMEM((N, 16, TILE), f32),
                pltpu.VMEM((16, TILE), f32),
                pltpu.VMEM((16, TILE), f32),
                pltpu.VMEM((8, TILE), f32),
                pltpu.VMEM((8, TILE), f32),
                pltpu.VMEM((N, 8, TILE), f32),
                pltpu.VMEM((N, 8, TILE), f32),
                pltpu.VMEM((group, 8, plane), f32),
                pltpu.VMEM((group, 8, plane), f32),
                pltpu.VMEM((ITERS, S, 8, TILE), f32),
                pltpu.VMEM((16, 16), f32),
                pltpu.VMEM((16, 16), f32),
                dma((len(small),)), dma((nvx,)), dma((nvx,)), dma((group, N)), dma((group, N)),
                dma((N,)), dma((N,)), dma((N,)), dma(()), dma((N,)), dma(()),
                dma((N,)), dma((N,)), dma((N,)), dma((N,)),
                dma((group,)), dma((group,)), dma((ITERS, S)), dma((ITERS, S)),
            ],
            compiler_params=pltpu.CompilerParams(
                collective_id=0, has_side_effects=True, vmem_limit_bytes=GRANT),
        )(velocity_dist, *small)
        return pl.pallas_call(
            lambda *refs: result_kernel(members, *refs),
            grid=(nvx,),
            out_shape=(jax.ShapeDtypeStruct((V, L), bf16), jax.ShapeDtypeStruct(macro_state.shape, f32)),
            in_specs=[
                pl.BlockSpec((plane, L), lambda j: (j, 0)),
                pl.BlockSpec((1, 2 * L, L), lambda j: (j, 0, 0)),
                pl.BlockSpec((1, 48, L), lambda j: (j, 0, 0)),
                vmem, vmem, vmem,
            ],
            out_specs=(pl.BlockSpec((plane, L), lambda j: (j, 0)), vmem),
            compiler_params=pltpu.CompilerParams(vmem_limit_bytes=GRANT),
        )(velocity_dist, band, zc, halo, macro, jnp.asarray(table["phi"]))

    placed = (P("vel", "space"), P(None, ("space", "vel")), P("space"), P("space"), P(), P())
    return jax.shard_map(
        per_device,
        mesh=mesh,
        in_specs=placed,
        out_specs=(P("vel", "space"), P(None, ("space", "vel"))),
        check_vma=False,
    )
```
